32 devices in a mesh: groups: 2 (over x), row: 16 (over z, y, core).
Axes of the slice: x: 2, y: 2, z: 4, core: 2. Of those that a mesh axis runs over, the one named last changes fastest.
Arguments:
- charges: bfloat16 [65536, 128], P(('groups', 'row')), parts along dimension 0, may hold values from -6 to 6
- cotangent: bfloat16 [65536, 128], P(('groups', 'row')), parts along dimension 0, may hold values from -6 to 6
- spread_weight: bfloat16 [1024, 128, 960], P(('groups', 'row')), parts along dimension 0, may hold values from -0.5 to 0.5
- atom_list: int32 [1024, 128], P(('groups', 'row')), parts along dimension 0, may hold values from -1 to 2047, as said below
- filter_modes: float32 [256, 256, 4], replicated, may hold values from 0.25 to 2
- gain: float32 [128], replicated, may hold values from 0.5 to 2
Outputs:
- charge_grad: bfloat16 [65536, 128], P(('groups', 'row')), parts along dimension 0
- filter_grad: float32 [256, 256, 8], P('row', None, 'groups'), parts along dimension 2
- gain_grad: float32 [256], P('groups'), parts along dimension 0
The draws below stay inside these ranges and needn't reach their ends.
There are 2 independent parts, one for each index of `groups`. The reference program is written for one: setup_inputs(seed, part) draws one part's arguments, and reference() takes and returns one part's arrays. A program takes and returns all parts, laid end to end along the dimension named above; an argument that names none is the same for every part. Nothing has to cross between parts.
Inputs may be any that keep to these rules, and one draw needn't show every extreme that they name: `atom_list`: entries other than -1 index the 2048 atoms of the index of row that holds the pencil; each such atom stands in exactly one slot of that block of 32 pencils, and in every block some pencil has all 128 slots occupied.
All inputs are finite; a program needn't handle non-finite values.
Results may differ from the reference program's by a relative error of at most 0.0078.
Values may be sent and summed in bfloat16 or wider, within the bound.
A program may use at most 192 MiB of HBM per device.

```python
import math
import jax
import jax.numpy as jnp
from jax import lax

NX = 256
NY = 256
NZ = 4
C = 128
H = 2
BX = 8
SLOT = 128
ATOM_DEV = 2048
NPEN_DEV = 32
NPENCILS = 512
ATOMS = 32768
EXT = 960
N_ROW = 16


def draw_atom_list(key, part):
    key = jax.random.fold_in(key, 11)

    def one_block(block_key):
        first_key, second_key, third_key = jax.random.split(block_key, 3)
        total_slots = NPEN_DEV * SLOT
        chosen = jax.random.randint(first_key, (), 0, NPEN_DEV)
        slot_pencil = jnp.arange(total_slots, dtype=jnp.int32) // SLOT
        shuffled = jax.random.permutation(second_key, total_slots).astype(jnp.int32)
        scores = jnp.where(slot_pencil == chosen, -1 - jnp.arange(total_slots, dtype=jnp.int32), shuffled)
        ordering = jnp.argsort(scores, stable=True)
        taken = ordering[:ATOM_DEV]
        atoms_order = jax.random.permutation(third_key, ATOM_DEV).astype(jnp.int32)
        listing = jnp.full((total_slots,), -1, jnp.int32).at[taken].set(atoms_order)
        return listing.reshape(NPEN_DEV, SLOT)
    block_keys = jax.random.split(key, NPENCILS // NPEN_DEV)
    return jax.vmap(one_block)(block_keys).reshape(NPENCILS, SLOT)


def levels(stream_key, extent, cuts, low, high):
    level = 1.0
    for axis_at, shards_of in cuts:
        heights = jax.random.uniform(jax.random.fold_in(jax.random.fold_in(stream_key, 6), axis_at), (shards_of,), jnp.float32, low / len(cuts), high / len(cuts))
        level = level * jnp.repeat(jnp.exp(heights), extent[axis_at] // shards_of).reshape((-1,) + (1,) * (len(extent) - 1 - axis_at))
    return level


def bell_draw(own_key, dims, scale, most, pieces=(), held_as=jnp.bfloat16):
    loudness = levels(own_key, dims, pieces, -0.22, 0.18) if pieces else 1.0
    entries = jax.random.normal(own_key, dims, jnp.float32) * scale * loudness
    return jnp.minimum(jnp.maximum(entries, -most), most).astype(held_as)


def setup_inputs(seed: int = 0, part: int = 0) -> dict:
    streams_of = jax.random.split(jax.random.key(seed), 7)
    part_keys = jax.random.split(jax.random.fold_in(streams_of[6], part), 7)
    return {
        "charges": bell_draw(part_keys[0], (ATOMS, C), 1.0, 6.0, ((0, 16),)),
        "cotangent": bell_draw(part_keys[1], (ATOMS, C), 1.0, 6.0, ((0, 16),)),
        "spread_weight": bell_draw(part_keys[2], (NPENCILS, SLOT, EXT), SLOT ** -0.5, 0.5, ((0, 16),)),
        "atom_list": draw_atom_list(jax.random.fold_in(jax.random.fold_in(streams_of[6], part), 71), part),
        "filter_modes": jnp.clip(jnp.exp(jax.random.uniform(streams_of[4], (NX, NY, NZ), jnp.float32, math.log(0.25), math.log(2.0))), 0.25, 2.0),
        "gain": jnp.clip(jnp.exp(jax.random.uniform(streams_of[5], (C,), jnp.float32, math.log(0.5), math.log(2.0))), 0.5, 2.0),
    }


def wave_tables(length):
    counter = jnp.arange(length, dtype=jnp.int32)
    turns = counter[:, None] * counter[None, :] % length
    angle = turns.astype(jnp.float32) * (2.0 * math.pi / length)
    factor = 1.0 / math.sqrt(length)
    return ((jnp.cos(angle) * factor).astype(jnp.bfloat16), (jnp.sin(angle) * factor).astype(jnp.bfloat16))

def pencil_cells():
    y_local = NY // N_ROW
    pencil = jnp.arange(NPENCILS, dtype=jnp.int32)
    device_of = pencil // NPEN_DEV
    block_of = pencil % NPEN_DEV
    offset_x = jnp.arange(BX + 2 * H, dtype=jnp.int32)
    offset_y = jnp.arange(y_local + 2 * H, dtype=jnp.int32)
    planes = jnp.arange(NZ, dtype=jnp.int32)
    cells_x = (block_of[:, None] * BX - H + offset_x[None, :]) % NX
    cells_y = (device_of[:, None] * y_local - H + offset_y[None, :]) % NY
    flat = (cells_x[:, :, None, None] * NY + cells_y[:, None, :, None]) * NZ + planes[None, None, None, :]
    return flat.reshape(NPENCILS, EXT).astype(jnp.int32)

def wide(array):
    return array.astype(jnp.float32)

def along_y(table, operand):
    return jnp.einsum('ky,xyr->xkr', wide(table), wide(operand), precision=lax.Precision.HIGHEST)

def reference(charges, cotangent, spread_weight, atom_list, filter_modes, gain):
    cell_index = pencil_cells()
    device_of = (jnp.arange(NPENCILS, dtype=jnp.int32) // NPEN_DEV)[:, None]
    occupied = atom_list >= 0
    atom_rows = jnp.where(occupied, device_of * ATOM_DEV + atom_list, 0).astype(jnp.int32)
    slot_live = occupied.astype(jnp.bfloat16)[..., None]
    spread_f32 = wide(spread_weight)

    def spread(source):
        gathered = wide(jnp.take(source, atom_rows, axis=0) * slot_live)
        extended = jnp.einsum('pse,psc->pec', spread_f32, gathered, precision=lax.Precision.HIGHEST)
        total = jnp.zeros((NX * NY * NZ, C), jnp.float32).at[cell_index.reshape(-1)].add(extended.reshape(-1, C))
        return total.reshape(NX, NY, NZ, C).astype(jnp.bfloat16)
    cos_x, sin_x = wave_tables(NX)
    cos_y, sin_y = wave_tables(NY)
    forward_x = jnp.concatenate([cos_x, -sin_x], axis=0)
    inverse_x = jnp.concatenate([cos_x, -sin_x], axis=1)

    def forward(spread_grid):
        section = jnp.dot(wide(forward_x), wide(spread_grid).reshape(NX, -1), precision=lax.Precision.HIGHEST)
        section = section.astype(jnp.bfloat16).reshape(2, NX, NY, NZ * C)
        real_part = along_y(cos_y, section[0]) + along_y(sin_y, section[1])
        imag_part = along_y(cos_y, section[1]) - along_y(sin_y, section[0])
        return (real_part, imag_part)
    density_re, density_im = forward(spread(charges))
    spread_re, spread_im = forward(spread(cotangent))
    mode_product = (density_re * spread_re + density_im * spread_im).reshape(NX, NY, NZ, C)
    filter_grad = jnp.einsum('xyzc,c->xyz', mode_product, gain, precision=lax.Precision.HIGHEST)
    gain_grad = jnp.einsum('xyzc,xyz->c', mode_product, filter_modes, precision=lax.Precision.HIGHEST)
    scaling = (filter_modes[..., None] * gain).reshape(NX, NY, NZ * C)
    filtered_re = (scaling * spread_re).astype(jnp.bfloat16)
    filtered_im = (scaling * spread_im).astype(jnp.bfloat16)
    back_re = (along_y(cos_y, filtered_re) - along_y(sin_y, filtered_im)).astype(jnp.bfloat16)
    back_im = (along_y(cos_y, filtered_im) + along_y(sin_y, filtered_re)).astype(jnp.bfloat16)
    stacked = wide(jnp.stack([back_re, back_im])).reshape(2 * NX, -1)
    rho_grad = jnp.dot(wide(inverse_x), stacked, precision=lax.Precision.HIGHEST).astype(jnp.bfloat16)
    rho_grad = rho_grad.reshape(NX * NY * NZ, C)
    gathered = wide(jnp.take(rho_grad, cell_index, axis=0))
    slot_values = jnp.einsum('pse,pec->psc', spread_f32, gathered, precision=lax.Precision.HIGHEST)
    targets = jnp.where(occupied, device_of * ATOM_DEV + atom_list, ATOMS).astype(jnp.int32)
    charge_grad = jnp.zeros((ATOMS, C), jnp.float32).at[targets.reshape(-1)].add(slot_values.reshape(-1, C), mode='drop')
    return (charge_grad.astype(jnp.bfloat16), filter_grad, gain_grad)
```

```python
import functools
import math

import jax
import jax.numpy as jnp
import ml_dtypes
import numpy as np
from jax import lax
from jax.experimental import pallas as pl
from jax.experimental.pallas import tpu as pltpu
from jax.sharding import PartitionSpec as P

NX = 256
NY = 256
NZ = 4
C = 128
H = 2
BX = 8
HR = H * NZ
VMEM_LIMIT = 58 * 1024 * 1024
BF = jnp.bfloat16
F32 = jnp.float32


def wave_tables(length):
    counter = np.arange(length)
    turns = counter[:, None] * counter[None, :] % length
    angle = turns.astype(np.float32) * np.float32(2.0 * math.pi / length)
    factor = np.float32(1.0 / math.sqrt(length))
    return np.cos(angle) * factor, np.sin(angle) * factor


def packed_x_table(rows):
    cos_x, sin_x = wave_tables(NX)
    half = NX // 2
    re = cos_x[:half].copy()
    im = -sin_x[:half]
    im[0] = cos_x[half]
    k_local = half // rows
    both = np.stack([re.reshape(rows, k_local, NX), im.reshape(rows, k_local, NX)], axis=1)
    return both.reshape(NX, NX)


def params(steps=1):
    return pltpu.CompilerParams(
        dimension_semantics=("arbitrary",) * steps, vmem_limit_bytes=VMEM_LIMIT
    )


def full(shape):
    return pl.BlockSpec(shape, lambda *_: (0,) * len(shape))


def dot(a, b):
    return jnp.dot(a, b, preferred_element_type=F32)


def spread_kernel(group, span, atom_ref, source_ref, weight_ref, out_ref, first, second):
    step = pl.program_id(0)
    atoms = source_ref.shape[0]
    slots = weight_ref.shape[2]

    @pl.when(step == 0)
    def _():
        zero = jnp.zeros((2 * H * span, C), F32)
        first[0 : 2 * H * span] = zero
        second[0 : 2 * H * span] = zero

    lane = lax.broadcasted_iota(jnp.int32, (slots, 128), 1).astype(F32)
    marks = []
    for j in range(group):
        held = jnp.broadcast_to(atom_ref[step * group + j], (128, slots)).T
        marks.append(
            jnp.concatenate(
                [(held == lane + float(a)).astype(F32).astype(BF) for a in range(0, atoms, 128)], axis=1
            )
        )
    gathered = dot(jnp.concatenate(marks, axis=0), source_ref[...]).astype(BF)
    for j in range(group):
        ext = dot(weight_ref[j], gathered[j * slots : (j + 1) * slots])
        base = pl.multiple_of((step * group + j) * (BX * span), 8)
        for half, total in enumerate((first, second)):
            part = ext[:, half * C : (half + 1) * C]
            total[pl.ds(base, 2 * H * span)] += part[: 2 * H * span]
            total[pl.ds(pl.multiple_of(base + 2 * H * span, 8), BX * span)] = part[2 * H * span :]

    @pl.when(step == pl.num_programs(0) - 1)
    def _():
        for half, total in enumerate((first, second)):
            total[NX * span : (NX + H) * span] += total[0 : H * span]
            total[H * span : 2 * H * span] += total[(NX + H) * span : (NX + 2 * H) * span]

            def move(r, _):
                out_ref[r, :, half * C : (half + 1) * C] = total[
                    pl.ds(H * span + r, NX, stride=span), :
                ].astype(BF)
                return 0

            lax.fori_loop(0, span, move, 0)


def spread(atom_rows, source, weight, span):
    pencils, ext, slots = weight.shape
    group = 4
    return pl.pallas_call(
        functools.partial(spread_kernel, group, span),
        grid=(pencils // group,),
        in_specs=[
            full(atom_rows.shape),
            full(source.shape),
            pl.BlockSpec((group, ext, slots), lambda i: (i, 0, 0)),
        ],
        out_specs=full((span, NX, 2 * C)),
        out_shape=jax.ShapeDtypeStruct((span, NX, 2 * C), BF),
        scratch_shapes=[pltpu.VMEM(((NX + 2 * H) * span, C), F32)] * 2,
        compiler_params=params(),
        cost_estimate=pl.CostEstimate(flops=7 * 10**9, bytes_accessed=24 * 10**6, transcendentals=0),
    )(atom_rows, source, weight)


def forward_x_kernel(y_local, table_ref, ext_ref, below_ref, above_ref, out_ref, wide):
    inner = y_local * NZ

    def put(r, value):
        place = (r % NZ) * y_local + r // NZ
        wide[pl.ds(place, NX, stride=inner + 1), :] = value

    def run(start, stop, extra):
        def body(i, _):
            r = start + 2 * i
            values = []
            for u in range(2):
                value = ext_ref[HR + r + u]
                if extra is not None:
                    value = (value.astype(F32) + extra(r + u).astype(F32)).astype(BF)
                values.append(value)
            result = dot(table_ref[...], jnp.concatenate(values, axis=1))
            put(r, result[:, :C])
            put(r + 1, result[:, C:])
            return 0

        if stop > start:
            lax.fori_loop(0, (stop - start) // 2, body, 0)

    run(0, HR, lambda r: below_ref[r])
    run(HR, inner - HR, None)
    run(inner - HR, inner, lambda r: above_ref[r - (inner - HR)])

    def cast(i, _):
        for u in range(8):
            k = i * 8 + u
            out_ref[pl.ds(pl.multiple_of(k * inner, 16), inner)] = wide[
                pl.ds(k * (inner + 1), inner)
            ].astype(BF)
        return 0

    lax.fori_loop(0, NX // 8, cast, 0)


def forward_x(table, ext, below, above, which, y_local):
    span = ext.shape[0]
    inner = y_local * NZ
    pick = lambda n: pl.BlockSpec((n, NX, C), lambda i: (0, 0, which))
    return pl.pallas_call(
        functools.partial(forward_x_kernel, y_local),
        grid=(1,),
        in_specs=[full((NX, NX)), pick(span), pick(HR), pick(HR)],
        out_specs=full((NX * inner, C)),
        out_shape=jax.ShapeDtypeStruct((NX * inner, C), BF),
        scratch_shapes=[pltpu.VMEM((NX * (inner + 1), C), F32)],
        compiler_params=params(),
        cost_estimate=pl.CostEstimate(flops=10**9, bytes_accessed=12 * 10**6, transcendentals=0),
    )(table, ext, below, above)


def modes_kernel(fwd_ref, inv_ref, flag_ref, gain_ref, filt_ref, last_ref, density_ref, grad_ref,
                 back_ref, fgrad_ref, flast_ref, ggrad_ref):
    step = pl.program_id(0)
    gain = gain_ref[...]

    @pl.when(step == 0)
    def _():
        ggrad_ref[...] = jnp.zeros_like(ggrad_ref)

    def load(ref, part, z):
        return ref[:, part, 0, z].reshape(NY, C)

    def store(part, z, value):
        back_ref[:, part, 0, z] = value.astype(BF).reshape(back_ref.shape[0], back_ref.shape[4], C)

    def run(parts, weight):
        weight = jnp.concatenate([weight, jnp.zeros((128 - NZ, NY), F32)], axis=0).T
        columns, filtered, total = [], [], jnp.zeros((1, C), F32)
        for z in range(NZ):
            d_re, d_im, g_re, g_im = parts(z)
            stacked = jnp.concatenate(
                [jnp.concatenate([d_re, g_re], axis=1), jnp.concatenate([d_im, g_im], axis=1)], axis=0
            )
            hat = dot(fwd_ref[...], stacked)
            dr, di = hat[:NY, :C], hat[NY:, :C]
            gr, gi = hat[:NY, C:], hat[NY:, C:]
            product = dr * gr + di * gi
            filt = weight[:, z : z + 1]
            columns.append(jnp.sum(product * gain, axis=1, keepdims=True))
            total = total + jnp.sum(product * filt, axis=0, keepdims=True)
            scaling = filt * gain
            filtered.append(
                jnp.concatenate([(scaling * gr).astype(BF), (scaling * gi).astype(BF)], axis=0)
            )
        ggrad_ref[...] += jnp.broadcast_to(total, ggrad_ref.shape)
        back = []
        for z in range(0, NZ, 2):
            both = dot(inv_ref[...], jnp.concatenate(filtered[z : z + 2], axis=1))
            back += [both[:, :C], both[:, C:]]
        columns.append(jnp.zeros((NY, 128 - NZ), F32))
        return jnp.concatenate(columns, axis=1).T[:NZ], back

    @pl.when(step > 0)
    def _():
        def parts(z):
            return (load(density_ref, 0, z), load(density_ref, 1, z),
                    load(grad_ref, 0, z), load(grad_ref, 1, z))

        columns, back = run(parts, filt_ref[0])
        fgrad_ref[0] = columns
        for z in range(NZ):
            store(0, z, back[z][:NY])
            store(1, z, back[z][NY:])

    @pl.when(step == 0)
    def _():
        flag = flag_ref[...]
        other = 1.0 - flag
        flag_b, other_b = flag.astype(BF), other.astype(BF)

        def parts(z):
            return (load(density_ref, 0, z), load(density_ref, 1, z) * other_b,
                    load(grad_ref, 0, z), load(grad_ref, 1, z) * other_b)

        columns, back = run(parts, filt_ref[0])
        fgrad_ref[0] = columns

        def last_parts(z):
            zero = jnp.zeros((NY, C), BF)
            return (load(density_ref, 1, z) * flag_b, zero, load(grad_ref, 1, z) * flag_b, zero)

        columns, last = run(last_parts, last_ref[...])
        flast_ref[...] = columns
        for z in range(NZ):
            store(0, z, back[z][:NY])
            store(1, z, back[z][NY:] * other + last[z][:NY] * flag)


def modes(fwd, inv, flag, gain, filt, last, density, grad):
    sources, _, k_local, _, y_rows, _ = density.shape
    block = pl.BlockSpec((sources, 2, 1, NZ, y_rows, C), lambda i: (0, 0, i, 0, 0, 0))
    column = pl.BlockSpec((1, NZ, NY), lambda i: (i, 0, 0))
    return pl.pallas_call(
        modes_kernel,
        grid=(k_local,),
        in_specs=[full(fwd.shape), full(inv.shape), full((1, C)), full((1, C)), column,
                  full((NZ, NY)), block, block],
        out_specs=[block, column, full((NZ, NY)), full((8, C))],
        out_shape=[
            jax.ShapeDtypeStruct(density.shape, BF),
            jax.ShapeDtypeStruct((k_local, NZ, NY), F32),
            jax.ShapeDtypeStruct((NZ, NY), F32),
            jax.ShapeDtypeStruct((8, C), F32),
        ],
        compiler_params=params(),
        cost_estimate=pl.CostEstimate(flops=10 * 10**9, bytes_accessed=14 * 10**6, transcendentals=0),
    )(fwd, inv, flag, gain, filt, last, density, grad)


def inverse_x_kernel(y_local, table_ref, in_ref, out_ref, wide, result):
    inner = y_local * NZ

    def widen(i, _):
        for u in range(8):
            k = i * 8 + u
            wide[pl.ds(k * (inner + 1), inner)] = in_ref[
                pl.ds(pl.multiple_of(k * inner, 16), inner)
            ].astype(F32)
        return 0

    lax.fori_loop(0, NX // 8, widen, 0)

    def body(i, _):
        values = []
        for u in range(2):
            r = 2 * i + u
            place = (r % NZ) * y_local + r // NZ
            values.append(wide[pl.ds(place, NX, stride=inner + 1), :].astype(BF))
        both = dot(table_ref[...], jnp.concatenate(values, axis=1))
        result[pl.ds(2 * i, NX, stride=inner + 1), :] = both[:, :C]
        result[pl.ds(2 * i + 1, NX, stride=inner + 1), :] = both[:, C:]
        return 0

    lax.fori_loop(0, inner // 2, body, 0)

    def cast(i, _):
        for u in range(8):
            x = i * 8 + u
            out_ref[pl.ds(pl.multiple_of(x * inner, 16), inner)] = result[
                pl.ds(x * (inner + 1), inner)
            ].astype(BF)
        return 0

    lax.fori_loop(0, NX // 8, cast, 0)


def inverse_x(table, back, y_local):
    shape = (NX * y_local * NZ, C)
    return pl.pallas_call(
        functools.partial(inverse_x_kernel, y_local),
        grid=(1,),
        in_specs=[full((NX, NX)), full(shape)],
        out_specs=full(shape),
        out_shape=jax.ShapeDtypeStruct(shape, BF),
        scratch_shapes=[pltpu.VMEM((NX * (y_local * NZ + 1), C), F32)] * 2,
        compiler_params=params(),
        cost_estimate=pl.CostEstimate(flops=10**9, bytes_accessed=8 * 10**6, transcendentals=0),
    )(table, back)


def collect_kernel(group, span, atom_ref, weight_ref, rho_ref, below_ref, above_ref, out_ref, ext, total):
    step = pl.program_id(0)
    atoms = total.shape[0]
    slots = weight_ref.shape[2]

    @pl.when(step == 0)
    def _():
        def build(i, _):
            x = (i + NX - H) % NX
            rows = jnp.concatenate(
                [below_ref[x].astype(F32), rho_ref[x].astype(F32), above_ref[x].astype(F32)], axis=0
            )
            ext[pl.ds(pl.multiple_of(i * span, 16), span)] = rows.astype(BF)
            return 0

        lax.fori_loop(0, NX + 2 * H, build, 0)
        total[...] = jnp.zeros_like(total)

    marks, values = [], []
    row = lax.broadcasted_iota(jnp.int32, (atoms, slots), 0).astype(F32)
    for j in range(group):
        p = step * group + j
        cells = ext[pl.ds(pl.multiple_of(p * (BX * span), 16), (BX + 2 * H) * span)]
        value = lax.dot_general(
            weight_ref[j], cells, (((0,), (0,)), ((), ())), preferred_element_type=F32
        )
        values.append(value.astype(BF))
        marks.append((row == atom_ref[p]).astype(F32).astype(BF))
    total[...] += dot(jnp.concatenate(marks, axis=1), jnp.concatenate(values, axis=0))

    @pl.when(step == pl.num_programs(0) - 1)
    def _():
        out_ref[...] = total[...].astype(BF)


def collect(atom_rows, weight, rho, below, above, atoms, span):
    pencils, ext, slots = weight.shape
    group = 4
    return pl.pallas_call(
        functools.partial(collect_kernel, group, span),
        grid=(pencils // group,),
        in_specs=[
            full(atom_rows.shape),
            pl.BlockSpec((group, ext, slots), lambda i: (i, 0, 0)),
            full(rho.shape),
            full(below.shape),
            full(above.shape),
        ],
        out_specs=full((atoms, C)),
        out_shape=jax.ShapeDtypeStruct((atoms, C), BF),
        scratch_shapes=[
            pltpu.VMEM(((NX + 2 * H) * span, C), BF),
            pltpu.VMEM((atoms, C), F32),
        ],
        compiler_params=params(),
        cost_estimate=pl.CostEstimate(flops=4 * 10**9, bytes_accessed=14 * 10**6, transcendentals=0),
    )(atom_rows, weight, rho, below, above)


def from_behind(value, axis, steps):
    count = lax.axis_size(axis)
    return lax.ppermute(value, axis, [(source, (source + steps) % count) for source in range(count)])


def flip_modes(modes_rows):
    return jnp.roll(jnp.flip(modes_rows, axis=-1), 1, axis=-1)


def local(charges, cotangent, spread_weight, atom_list, filter_modes, gain):
    rows = lax.axis_size("row")
    me = lax.axis_index("row")
    pencils = spread_weight.shape[0]
    atoms = charges.shape[0]
    y_local = NY // rows
    half = NX // 2
    k_local = half // rows
    inner = y_local * NZ
    span = inner + 2 * HR
    cos_y, sin_y = wave_tables(NY)
    packed = packed_x_table(rows)
    as_table = lambda t: jnp.asarray(t.astype(ml_dtypes.bfloat16))
    fwd_x = as_table(packed)
    inv_x = as_table(packed.T)
    fwd_y = as_table(np.block([[cos_y, sin_y], [-sin_y, cos_y]]))
    inv_y = as_table(np.block([[cos_y, -sin_y], [sin_y, cos_y]]))
    atom_rows = atom_list.astype(F32)[:, None, :]
    weight = spread_weight.transpose(0, 2, 1)

    ext = spread(atom_rows, jnp.concatenate([charges, cotangent], axis=1), weight, span)
    below = from_behind(ext[span - HR :], "row", 1)
    above = from_behind(ext[:HR], "row", -1)

    def exchange(cells):
        return lax.all_to_all(cells, "row", split_axis=0, concat_axis=0, tiled=True)

    def by_owner(grid):
        got = exchange(grid.reshape(rows, 2 * k_local, NZ, y_local, C))
        got = got.reshape(rows, 2, k_local, NZ, y_local, C)
        if y_local % 16:
            got = got.transpose(1, 2, 3, 0, 4, 5).reshape(1, 2, k_local, NZ, NY, C)
        return got

    density = by_owner(forward_x(fwd_x, ext, below, above, 0, y_local))
    grad = by_owner(forward_x(fwd_x, ext, below, above, 1, y_local))

    own = me * k_local
    filter_modes = filter_modes.transpose(0, 2, 1)
    straight = lax.dynamic_slice_in_dim(filter_modes, own, k_local, 0)
    mirrored = flip_modes(filter_modes)
    ks = own + jnp.arange(k_local)
    opposite = jnp.take(mirrored, (NX - ks) % NX, axis=0)
    filt = straight + jnp.where((ks == 0)[:, None, None], 0.0, opposite)
    flag = jnp.broadcast_to((me == 0).astype(F32), (1, C))
    back, fgrad, flast, ggrad = modes(
        fwd_y, inv_y, flag, gain[None, :], filt, filter_modes[half], density, grad
    )
    small = jnp.concatenate([fgrad.reshape(-1, C), flast.reshape(-1, C), ggrad], axis=0)
    shared = lax.all_gather(small, "row")
    if y_local % 16:
        back = back.reshape(2, k_local, NZ, rows, y_local, C).transpose(3, 0, 1, 2, 4, 5)
    back = exchange(back.reshape(rows, 2 * k_local, NZ, y_local, C))
    rho = inverse_x(inv_x, back.reshape(NX * inner, C), y_local).reshape(NX, inner, C)
    below = from_behind(rho[:, inner - HR :], "row", 1)
    above = from_behind(rho[:, :HR], "row", -1)
    charge_grad = collect(atom_rows, weight, rho, below, above, atoms, span)

    plane = NY * NZ // C
    body = shared[:, : k_local * plane].reshape(half, NZ, NY)
    last = shared[0, k_local * plane : (k_local + 1) * plane].reshape(1, NZ, NY)
    gain_grad = jnp.sum(shared[:, (k_local + 1) * plane], axis=0)
    known = jnp.concatenate([body, last], axis=0)
    mine = me * (NX // rows) + jnp.arange(NX // rows)
    picked = jnp.take(known, jnp.where(mine <= half, mine, NX - mine), axis=0)
    filter_grad = jnp.where((mine <= half)[:, None, None], picked, flip_modes(picked))
    return (charge_grad, filter_grad.transpose(0, 2, 1), gain_grad)


def solution(mesh):
    placed = (
        P(("groups", "row"), None),
        P(("groups", "row"), None),
        P(("groups", "row"), None, None),
        P(("groups", "row"), None),
        P(),
        P(),
    )
    return jax.shard_map(
        local,
        mesh=mesh,
        in_specs=placed,
        out_specs=(P(("groups", "row"), None), P("row", None, "groups"), P("groups")),
        check_vma=False,
    )
```

```python
import functools
import math

import jax
import jax.numpy as jnp
import ml_dtypes
import numpy as np
from jax import lax
from jax.experimental import pallas as pl
from jax.experimental.pallas import tpu as pltpu
from jax.sharding import PartitionSpec as P

NX = 256
NY = 256
NZ = 4
C = 128
H = 2
BX = 8
HR = H * NZ
VMEM_LIMIT = 58 * 1024 * 1024
BF = jnp.bfloat16
F32 = jnp.float32


def wave_tables(length):
    counter = np.arange(length)
    turns = counter[:, None] * counter[None, :] % length
    angle = turns.astype(np.float32) * np.float32(2.0 * math.pi / length)
    factor = np.float32(1.0 / math.sqrt(length))
    return np.cos(angle) * factor, np.sin(angle) * factor


def packed_x_table(rows):
    cos_x, sin_x = wave_tables(NX)
    half = NX // 2
    re = cos_x[:half].copy()
    im = -sin_x[:half]
    im[0] = cos_x[half]
    k_local = half // rows
    both = np.stack([re.reshape(rows, k_local, NX), im.reshape(rows, k_local, NX)], axis=1)
    return both.reshape(NX, NX)


def params(steps=1):
    return pltpu.CompilerParams(
        dimension_semantics=("arbitrary",) * steps, vmem_limit_bytes=VMEM_LIMIT
    )


def full(shape):
    return pl.BlockSpec(shape, lambda *_: (0,) * len(shape))


def dot(a, b):
    return jnp.dot(a, b, preferred_element_type=F32)


def spread_kernel(group, span, pitch, atom_ref, source_ref, weight_ref, out_ref, total):
    step = pl.program_id(0)
    atoms = source_ref.shape[0]
    slots = weight_ref.shape[2]

    @pl.when(step == 0)
    def _():
        total[0 : 2 * H * pitch] = jnp.zeros((2 * H * pitch, C), F32)

    lane = lax.broadcasted_iota(jnp.int32, (slots, 128), 1).astype(F32)
    marks = []
    for j in range(group):
        held = jnp.broadcast_to(atom_ref[step * group + j], (128, slots)).T
        marks.append(
            jnp.concatenate(
                [(held == lane + float(a)).astype(F32).astype(BF) for a in range(0, atoms, 128)], axis=1
            )
        )
    gathered = dot(jnp.concatenate(marks, axis=0), source_ref[...]).astype(BF)
    for j in range(group):
        ext = dot(weight_ref[j], gathered[j * slots : (j + 1) * slots])
        base = (step * group + j) * (BX * pitch)
        for x in range(BX + 2 * H):
            at = pl.ds(pl.multiple_of(base + x * pitch, 8), span)
            part = ext[x * span : (x + 1) * span]
            if x < 2 * H:
                total[at] += part
            else:
                total[at] = part

    @pl.when(step == pl.num_programs(0) - 1)
    def _():
        total[NX * pitch : (NX + H) * pitch] += total[0 : H * pitch]
        total[H * pitch : 2 * H * pitch] += total[(NX + H) * pitch : (NX + 2 * H) * pitch]

        def move(r, _):
            out_ref[r] = total[pl.ds(H * pitch + r, NX, stride=pitch), :].astype(BF)
            return 0

        lax.fori_loop(0, span, move, 0)


def spread(atom_rows, source, weight, span):
    pencils, ext, slots = weight.shape
    group = 4
    pitch = span + 8
    return pl.pallas_call(
        functools.partial(spread_kernel, group, span, pitch),
        grid=(pencils // group,),
        in_specs=[
            full(atom_rows.shape),
            full(source.shape),
            pl.BlockSpec((group, ext, slots), lambda i: (i, 0, 0)),
        ],
        out_specs=full((span, NX, C)),
        out_shape=jax.ShapeDtypeStruct((span, NX, C), BF),
        scratch_shapes=[pltpu.VMEM(((NX + 2 * H) * pitch, C), F32)],
        compiler_params=params(),
        cost_estimate=pl.CostEstimate(flops=4 * 10**9, bytes_accessed=14 * 10**6, transcendentals=0),
    )(atom_rows, source, weight)


def forward_x_kernel(y_local, table_ref, ext_ref, below_ref, above_ref, out_ref, wide):
    inner = y_local * NZ

    def put(r, value):
        place = (r % NZ) * y_local + r // NZ
        wide[pl.ds(place, NX, stride=inner + 1), :] = value

    def run(start, stop, extra):
        def body(i, _):
            r = start + 2 * i
            values = []
            for u in range(2):
                value = ext_ref[HR + r + u]
                if extra is not None:
                    value = (value.astype(F32) + extra(r + u).astype(F32)).astype(BF)
                values.append(value)
            result = dot(table_ref[...], jnp.concatenate(values, axis=1))
            put(r, result[:, :C])
            put(r + 1, result[:, C:])
            return 0

        if stop > start:
            lax.fori_loop(0, (stop - start) // 2, body, 0)

    run(0, HR, lambda r: below_ref[r])
    run(HR, inner - HR, None)
    run(inner - HR, inner, lambda r: above_ref[r - (inner - HR)])

    def cast(i, _):
        for u in range(8):
            k = i * 8 + u
            out_ref[pl.ds(pl.multiple_of(k * inner, 16), inner)] = wide[
                pl.ds(k * (inner + 1), inner)
            ].astype(BF)
        return 0

    lax.fori_loop(0, NX // 8, cast, 0)


def forward_x(table, ext, below, above, y_local):
    span = ext.shape[0]
    inner = y_local * NZ
    return pl.pallas_call(
        functools.partial(forward_x_kernel, y_local),
        grid=(1,),
        in_specs=[full((NX, NX)), full((span, NX, C)), full((HR, NX, C)), full((HR, NX, C))],
        out_specs=full((NX * inner, C)),
        out_shape=jax.ShapeDtypeStruct((NX * inner, C), BF),
        scratch_shapes=[pltpu.VMEM((NX * (inner + 1), C), F32)],
        compiler_params=params(),
        cost_estimate=pl.CostEstimate(flops=10**9, bytes_accessed=12 * 10**6, transcendentals=0),
    )(table, ext, below, above)


def modes_kernel(fwd_ref, inv_ref, flag_ref, gain_ref, filt_ref, last_ref, density_ref, grad_ref,
                 back_ref, fgrad_ref, flast_ref, ggrad_ref):
    step = pl.program_id(0)
    gain = gain_ref[...]

    @pl.when(step == 0)
    def _():
        ggrad_ref[...] = jnp.zeros_like(ggrad_ref)

    def load(ref, part, z):
        return ref[:, part, 0, z].reshape(NY, C)

    def store(part, z, value):
        back_ref[:, part, 0, z] = value.astype(BF).reshape(back_ref.shape[0], back_ref.shape[4], C)

    def run(parts, weight):
        weight = jnp.concatenate([weight, jnp.zeros((128 - NZ, NY), F32)], axis=0).T
        columns, filtered, total = [], [], jnp.zeros((1, C), F32)
        for z in range(NZ):
            d_re, d_im, g_re, g_im = parts(z)
            stacked = jnp.concatenate(
                [jnp.concatenate([d_re, g_re], axis=1), jnp.concatenate([d_im, g_im], axis=1)], axis=0
            )
            hat = dot(fwd_ref[...], stacked)
            dr, di = hat[:NY, :C], hat[NY:, :C]
            gr, gi = hat[:NY, C:], hat[NY:, C:]
            product = dr * gr + di * gi
            filt = weight[:, z : z + 1]
            columns.append(jnp.sum(product * gain, axis=1, keepdims=True))
            total = total + jnp.sum(product * filt, axis=0, keepdims=True)
            scaling = filt * gain
            filtered.append(
                jnp.concatenate([(scaling * gr).astype(BF), (scaling * gi).astype(BF)], axis=0)
            )
        ggrad_ref[...] += jnp.broadcast_to(total, ggrad_ref.shape)
        back = []
        for z in range(0, NZ, 2):
            both = dot(inv_ref[...], jnp.concatenate(filtered[z : z + 2], axis=1))
            back += [both[:, :C], both[:, C:]]
        columns.append(jnp.zeros((NY, 128 - NZ), F32))
        return jnp.concatenate(columns, axis=1).T[:NZ], back

    @pl.when(step > 0)
    def _():
        def parts(z):
            return (load(density_ref, 0, z), load(density_ref, 1, z),
                    load(grad_ref, 0, z), load(grad_ref, 1, z))

        columns, back = run(parts, filt_ref[0])
        fgrad_ref[0] = columns
        for z in range(NZ):
            store(0, z, back[z][:NY])
            store(1, z, back[z][NY:])

    @pl.when(step == 0)
    def _():
        flag = flag_ref[...]
        other = 1.0 - flag
        flag_b, other_b = flag.astype(BF), other.astype(BF)

        def parts(z):
            return (load(density_ref, 0, z), load(density_ref, 1, z) * other_b,
                    load(grad_ref, 0, z), load(grad_ref, 1, z) * other_b)

        columns, back = run(parts, filt_ref[0])
        fgrad_ref[0] = columns

        def last_parts(z):
            zero = jnp.zeros((NY, C), BF)
            return (load(density_ref, 1, z) * flag_b, zero, load(grad_ref, 1, z) * flag_b, zero)

        columns, last = run(last_parts, last_ref[...])
        flast_ref[...] = columns
        for z in range(NZ):
            store(0, z, back[z][:NY])
            store(1, z, back[z][NY:] * other + last[z][:NY] * flag)


def modes(fwd, inv, flag, gain, filt, last, density, grad):
    sources, _, k_local, _, y_rows, _ = density.shape
    block = pl.BlockSpec((sources, 2, 1, NZ, y_rows, C), lambda i: (0, 0, i, 0, 0, 0))
    column = pl.BlockSpec((1, NZ, NY), lambda i: (i, 0, 0))
    return pl.pallas_call(
        modes_kernel,
        grid=(k_local,),
        in_specs=[full(fwd.shape), full(inv.shape), full((1, C)), full((1, C)), column,
                  full((NZ, NY)), block, block],
        out_specs=[block, column, full((NZ, NY)), full((8, C))],
        out_shape=[
            jax.ShapeDtypeStruct(density.shape, BF),
            jax.ShapeDtypeStruct((k_local, NZ, NY), F32),
            jax.ShapeDtypeStruct((NZ, NY), F32),
            jax.ShapeDtypeStruct((8, C), F32),
        ],
        compiler_params=params(),
        cost_estimate=pl.CostEstimate(flops=10 * 10**9, bytes_accessed=14 * 10**6, transcendentals=0),
    )(fwd, inv, flag, gain, filt, last, density, grad)


def inverse_x_kernel(y_local, pitch, starts, count, out_pitch, table_ref, in_ref, *rest):
    outs, wide, result = rest[:-2], rest[-2], rest[-1]
    inner = y_local * NZ

    def widen(i, _):
        for u in range(8):
            k = i * 8 + u
            wide[pl.ds(pl.multiple_of(k * pitch, 8), inner)] = in_ref[
                pl.ds(pl.multiple_of(k * inner, 16), inner)
            ].astype(F32)
        return 0

    lax.fori_loop(0, NX // 8, widen, 0)
    for start, out_ref in zip(starts, outs):

        def body(i, _):
            values = []
            for u in range(2):
                r = start + 2 * i + u
                place = (r % NZ) * y_local + r // NZ
                values.append(wide[pl.ds(place, NX, stride=pitch), :].astype(BF))
            both = dot(table_ref[...], jnp.concatenate(values, axis=1))
            result[pl.ds(2 * i, NX, stride=out_pitch), :] = both[:, :C]
            result[pl.ds(2 * i + 1, NX, stride=out_pitch), :] = both[:, C:]
            return 0

        lax.fori_loop(0, count // 2, body, 0)

        def cast(i, _):
            for u in range(8):
                x = i * 8 + u
                out_ref[x] = result[pl.ds(pl.multiple_of(x * out_pitch, 8), count)].astype(BF)
            return 0

        lax.fori_loop(0, NX // 8, cast, 0)


def inverse_x(table, back, y_local, starts, count):
    inner = y_local * NZ
    pitch = inner + 8
    out_pitch = (count // 8 + 1 - count // 8 % 2) * 8
    return pl.pallas_call(
        functools.partial(inverse_x_kernel, y_local, pitch, starts, count, out_pitch),
        grid=(1,),
        in_specs=[full((NX, NX)), full((NX * inner, C))],
        out_specs=[full((NX, count, C))] * len(starts),
        out_shape=[jax.ShapeDtypeStruct((NX, count, C), BF)] * len(starts),
        scratch_shapes=[pltpu.VMEM((NX * pitch, C), F32), pltpu.VMEM((NX * out_pitch, C), F32)],
        compiler_params=params(),
        cost_estimate=pl.CostEstimate(
            flops=10**9 * count * len(starts) // inner, bytes_accessed=8 * 10**6, transcendentals=0
        ),
    )(table, back)


def collect_kernel(group, span, atom_ref, weight_ref, rho_ref, below_ref, above_ref, out_ref, ext, total):
    step = pl.program_id(0)
    atoms = total.shape[0]
    slots = weight_ref.shape[2]

    @pl.when(step == 0)
    def _():
        def build(i, _):
            x = (i + NX - H) % NX
            rows = jnp.concatenate(
                [below_ref[x].astype(F32), rho_ref[x].astype(F32), above_ref[x].astype(F32)], axis=0
            )
            ext[pl.ds(pl.multiple_of(i * span, 16), span)] = rows.astype(BF)
            return 0

        lax.fori_loop(0, NX + 2 * H, build, 0)
        total[...] = jnp.zeros_like(total)

    marks, values = [], []
    row = lax.broadcasted_iota(jnp.int32, (atoms, slots), 0).astype(F32)
    for j in range(group):
        p = step * group + j
        cells = ext[pl.ds(pl.multiple_of(p * (BX * span), 16), (BX + 2 * H) * span)]
        value = lax.dot_general(
            weight_ref[j], cells, (((0,), (0,)), ((), ())), preferred_element_type=F32
        )
        values.append(value.astype(BF))
        marks.append((row == atom_ref[p]).astype(F32).astype(BF))
    total[...] += dot(jnp.concatenate(marks, axis=1), jnp.concatenate(values, axis=0))

    @pl.when(step == pl.num_programs(0) - 1)
    def _():
        out_ref[...] = total[...].astype(BF)


def collect(atom_rows, weight, rho, below, above, atoms, span):
    pencils, ext, slots = weight.shape
    group = 4
    return pl.pallas_call(
        functools.partial(collect_kernel, group, span),
        grid=(pencils // group,),
        in_specs=[
            full(atom_rows.shape),
            pl.BlockSpec((group, ext, slots), lambda i: (i, 0, 0)),
            full(rho.shape),
            full(below.shape),
            full(above.shape),
        ],
        out_specs=full((atoms, C)),
        out_shape=jax.ShapeDtypeStruct((atoms, C), BF),
        scratch_shapes=[
            pltpu.VMEM(((NX + 2 * H) * span, C), BF),
            pltpu.VMEM((atoms, C), F32),
        ],
        compiler_params=params(),
        cost_estimate=pl.CostEstimate(flops=4 * 10**9, bytes_accessed=14 * 10**6, transcendentals=0),
    )(atom_rows, weight, rho, below, above)


def from_behind(value, axis, steps):
    count = lax.axis_size(axis)
    return lax.ppermute(value, axis, [(source, (source + steps) % count) for source in range(count)])


def flip_modes(modes_rows):
    return jnp.roll(jnp.flip(modes_rows, axis=-1), 1, axis=-1)


def local(charges, cotangent, spread_weight, atom_list, filter_modes, gain):
    rows = lax.axis_size("row")
    me = lax.axis_index("row")
    pencils = spread_weight.shape[0]
    atoms = charges.shape[0]
    y_local = NY // rows
    half = NX // 2
    k_local = half // rows
    inner = y_local * NZ
    span = inner + 2 * HR
    cos_y, sin_y = wave_tables(NY)
    packed = packed_x_table(rows)
    as_table = lambda t: jnp.asarray(t.astype(ml_dtypes.bfloat16))
    fwd_x = as_table(packed)
    inv_x = as_table(packed.T)
    fwd_y = as_table(np.block([[cos_y, sin_y], [-sin_y, cos_y]]))
    inv_y = as_table(np.block([[cos_y, -sin_y], [sin_y, cos_y]]))
    atom_rows = atom_list.astype(F32)[:, None, :]
    weight = spread_weight.transpose(0, 2, 1)

    def halo(ext):
        return from_behind(ext[span - HR :], "row", 1), from_behind(ext[:HR], "row", -1)

    def exchange(cells):
        return lax.all_to_all(cells, "row", split_axis=0, concat_axis=0, tiled=True)

    def by_owner(grid):
        got = exchange(grid.reshape(rows, 2 * k_local, NZ, y_local, C))
        got = got.reshape(rows, 2, k_local, NZ, y_local, C)
        if y_local % 16:
            got = got.transpose(1, 2, 3, 0, 4, 5).reshape(1, 2, k_local, NZ, NY, C)
        return got

    density_ext = spread(atom_rows, charges, weight, span)
    density_halo = halo(density_ext)
    density_ext, later_rows = lax.optimization_barrier((density_ext, atom_rows))
    grad_ext = spread(later_rows, cotangent, weight, span)
    grad_halo = halo(grad_ext)
    density_x = forward_x(fwd_x, density_ext, *density_halo, y_local)
    density = by_owner(density_x)
    grad = by_owner(forward_x(fwd_x, grad_ext, *grad_halo, y_local))

    own = me * k_local
    filter_modes = filter_modes.transpose(0, 2, 1)
    straight = lax.dynamic_slice_in_dim(filter_modes, own, k_local, 0)
    mirrored = flip_modes(filter_modes)
    ks = own + jnp.arange(k_local)
    opposite = jnp.take(mirrored, (NX - ks) % NX, axis=0)
    filt = straight + jnp.where((ks == 0)[:, None, None], 0.0, opposite)
    flag = jnp.broadcast_to((me == 0).astype(F32), (1, C))
    back, fgrad, flast, ggrad = modes(
        fwd_y, inv_y, flag, gain[None, :], filt, filter_modes[half], density, grad
    )
    gains = lax.all_gather(ggrad, "row")
    half_rows = rows // 2
    even_first = [(d, d // 2 if d % 2 == 0 else rows - (d + 1) // 2) for d in range(rows)]
    odd_first = [(d, d // 2 if d % 2 else rows - (d + 2) // 2) for d in range(rows)]
    single = [(2 * f % rows, rows - f) for f in range(1, half_rows + 1)]
    near = lax.ppermute(fgrad, "row", even_first)
    far = lax.ppermute(fgrad, "row", odd_first)
    edge = lax.ppermute(jnp.where(me == 0, flast, fgrad[0])[None], "row", single)
    if y_local % 16:
        back = back.reshape(2, k_local, NZ, rows, y_local, C).transpose(3, 0, 1, 2, 4, 5)
    back = exchange(back.reshape(rows, 2 * k_local, NZ, y_local, C))
    back, gains, near, far, edge = lax.optimization_barrier((back, gains, near, far, edge))
    gain_grad = jnp.sum(gains[:, 0], axis=0)
    straight_rows = jnp.concatenate([near, far], axis=0)
    turned_rows = jnp.concatenate([edge, near[::-1], far[::-1][: k_local - 1]], axis=0)
    filter_grad = jnp.where(me < half_rows, straight_rows, flip_modes(turned_rows))
    back = back.reshape(NX * inner, C)
    head, tail = inverse_x(inv_x, back, y_local, (0, inner - HR), HR)
    below = from_behind(tail, "row", 1)
    above = from_behind(head, "row", -1)
    (rho,) = inverse_x(inv_x, back, y_local, (0,), inner)
    charge_grad = collect(atom_rows, weight, rho, below, above, atoms, span)
    return (charge_grad, filter_grad.transpose(0, 2, 1), gain_grad)


def solution(mesh):
    placed = (
        P(("groups", "row"), None),
        P(("groups", "row"), None),
        P(("groups", "row"), None, None),
        P(("groups", "row"), None),
        P(),
        P(),
    )
    return jax.shard_map(
        local,
        mesh=mesh,
        in_specs=placed,
        out_specs=(P(("groups", "row"), None), P("row", None, "groups"), P("groups")),
        check_vma=False,
    )
```
